256 devices in a mesh: span: 4 (over z_hi), space: 64 (over x, y, z_lo, core).
Axes of the slice: x: 4, y: 4, z: 8 (z_hi: 4, z_lo: 2; z = z_hi * 2 + z_lo), core: 2. Of those that a mesh axis runs over, the one named last changes fastest.
Arguments:
- query: bfloat16 [4, 8192, 768], P('span', 'space'), may hold values from -130 to 130
- key: bfloat16 [4, 8192, 128], P('span', 'space'), may hold values from -5 to 5
- value: bfloat16 [4, 8192, 128], P('span', 'space'), may hold values from -6 to 6
- noise_step: int32 [4], replicated, may hold values from 0 to 63
- span_mask: int32 [4, 4], replicated, may hold values from 0 to 1, as said below
- gate_weight: float32 [256, 768], replicated, may hold values from -0.375 to 0.375
Outputs:
- attended: bfloat16 [4, 8192, 768], P('span', 'space')
The draws below stay inside these ranges and needn't reach their ends.
Inputs may be any that keep to these rules, and one draw needn't show every extreme that they name: span_mask is 1 on the diagonal and 0 above it.
All inputs are finite; a program needn't handle non-finite values.
Results may differ from the reference program's by a relative error of at most 0.0095.
Values may be sent and summed in bfloat16 or wider, within the bound.
No kernel may reach another device: no remote copies, remote signals or barrier semaphores. Data moves between devices by JAX's collectives and lax.ppermute only.
A program may use at most 64 MiB of HBM per device.

```python
import math
import jax
import jax.numpy as jnp
from jax import lax

HEAD = 128
QH = 6
EMB = 256
STEPS = 64
SPANS = 4
CTOK = 8192


def shared_keys(key):
    return jnp.clip(jax.random.normal(key, (SPANS, CTOK, HEAD), jnp.float32), -5.0, 5.0)


def draw_key(key, part):
    base = shared_keys(key)
    return base.astype(jnp.bfloat16)


def draw_query(key, part):
    key = jax.random.fold_in(key, 23)
    fresh = jnp.clip(jax.random.normal(key, (SPANS, CTOK, QH, HEAD), jnp.float32), -5.0, 5.0)
    return fresh.reshape(SPANS, CTOK, QH * HEAD).astype(jnp.bfloat16)


def draw_span_mask(key, part):
    key = jax.random.fold_in(key, 37)
    coins = jax.random.randint(key, (SPANS, SPANS), 0, 2)
    rows = jnp.arange(SPANS, dtype=jnp.int32)[:, None]
    cols = jnp.arange(SPANS, dtype=jnp.int32)[None, :]
    below = jnp.where(coins > 0, 1, 0)
    return jnp.where(rows == cols, 1, jnp.where(cols < rows, below, 0)).astype(jnp.int32)


def set_ends(entries, own_key, least, top_value):
    longest = entries.shape.index(max(entries.shape))
    spots = []
    for shift in (0, 1):
        where = [jax.random.randint(jax.random.fold_in(own_key, axis), (), 0, length) for axis, length in enumerate(entries.shape)]
        where[longest] = (where[longest] + shift) % entries.shape[longest]
        spots.append(tuple(where))
    return entries.at[spots[0]].set(least).at[spots[1]].set(top_value)


def block_scale(stream_key, extent, split, low, high):
    def one(position, parts):
        heights = jax.random.uniform(jax.random.fold_in(jax.random.fold_in(stream_key, 6), position), (parts,), jnp.float32, low / len(split), high / len(split))
        return jnp.repeat(jnp.exp(heights), extent[position] // parts).reshape((-1,) + (1,) * (len(extent) - position - 1))

    factor_of = one(*split[0])
    for cut in split[1:]:
        factor_of = factor_of * one(*cut)
    return factor_of


def gaussian(stream_key, dims, width, limit, split=(), kind=jnp.bfloat16):
    values = width * jax.random.normal(stream_key, dims, jnp.float32)
    if split:
        values = values * block_scale(stream_key, dims, split, -0.22, 0.18)
    return jnp.clip(values, -limit, limit).astype(kind)


def setup_inputs(seed: int = 0) -> dict:
    seeds = jax.random.split(jax.random.key(seed), 7)
    return {
        "query": draw_query(jax.random.fold_in(seeds[6], 71), 0),
        "key": draw_key(jax.random.fold_in(seeds[6], 71), 0),
        "value": gaussian(seeds[2], (SPANS, CTOK, HEAD), 1.0, 6.0, ((0, 4), (1, 64))),
        "noise_step": set_ends(jax.random.randint(seeds[3], (SPANS,), 0, STEPS), jax.random.fold_in(seeds[3], 1), 0, STEPS - 1).astype(jnp.int32),
        "span_mask": draw_span_mask(jax.random.fold_in(seeds[6], 71), 0),
        "gate_weight": gaussian(seeds[5], (EMB, QH * HEAD), EMB ** -0.5, 0.375, (), jnp.float32),
    }


def noise_gate(noise_step, gate_weight):
    half = EMB // 2
    freqs = jnp.exp(-math.log(10000.0) * jnp.arange(half, dtype=jnp.float32) / half)
    angles = noise_step.astype(jnp.float32)[:, None] * (1000.0 / STEPS) * freqs[None, :]
    embed = jnp.concatenate([jnp.cos(angles), jnp.sin(angles)], axis=1)
    return jax.nn.sigmoid(jnp.dot(embed, gate_weight, precision=lax.Precision.HIGHEST))

def reference(query, key, value, noise_step, span_mask, gate_weight):
    gate = noise_gate(noise_step, gate_weight)
    keys_all = key.reshape(SPANS * CTOK, HEAD).astype(jnp.float32)
    values_all = value.reshape(SPANS * CTOK, HEAD).astype(jnp.float32)
    span_ids = jnp.arange(SPANS * CTOK, dtype=jnp.int32) // CTOK
    block = math.gcd(CTOK, 512)
    scale = HEAD ** (-0.5)
    outputs = []
    for span in range(SPANS):
        allow = span_mask[span][span_ids] > 0
        queries = query[span].reshape(CTOK // block, block, QH, HEAD).astype(jnp.float32)

        def one_block(rows):
            scores = jnp.einsum('tqd,kd->tqk', rows, keys_all) * scale
            masked = jnp.where(allow[None, None, :], scores, -1e+30)
            top = lax.optimization_barrier(jnp.max(masked, axis=2, keepdims=True))
            probs = jnp.where(allow[None, None, :], jnp.exp(scores - top), 0.0)
            total = lax.optimization_barrier(jnp.sum(probs, axis=2))
            weights = probs.astype(jnp.bfloat16).astype(jnp.float32)
            mixed = jnp.einsum('tqk,kd->tqd', weights, values_all) / total[:, :, None]
            mixed = mixed.reshape(block, QH * HEAD)
            normed = mixed * lax.rsqrt(lax.optimization_barrier(jnp.mean(mixed * mixed, axis=1, keepdims=True)) + 1e-06)
            return (gate[span][None, :] * normed).astype(jnp.bfloat16)
        outputs.append(lax.map(one_block, queries).reshape(CTOK, QH * HEAD))
    return jnp.stack(outputs, axis=0)
```

```python
import functools
import math

import jax
import jax.numpy as jnp
from jax import lax
from jax.experimental import pallas as pl
from jax.experimental.pallas import tpu as pltpu
from jax.sharding import Mesh, PartitionSpec as P

STEPS = 64
NT = (((1,), (1,)), ((), ()))
F32 = jnp.float32
BF16 = jnp.bfloat16
SUM_LOW = 2.0**-100
SUM_HIGH = 2.0**100
VMEM = 56 << 20


def noise_gate(step_now, gate_weight, embed_width):
    half = embed_width // 2
    freqs = jnp.exp(-math.log(10000.0) * jnp.arange(half, dtype=F32) / half)
    angles = step_now.astype(F32)[:, None] * (1000.0 / STEPS) * freqs[None, :]
    embed = jnp.concatenate([jnp.cos(angles), jnp.sin(angles)], axis=1)
    return jax.nn.sigmoid(jnp.dot(embed, gate_weight, precision=lax.Precision.HIGHEST))


def lane_of(rows):
    return lax.broadcasted_iota(jnp.int32, (rows, 128), 1)


def add_blocks(count, q_ref, kv_refs, acc_ref, sum_ref, scale):
    tok = q_ref.shape[1]
    heads = q_ref.shape[2] // 128
    pair = 2 if heads % 2 == 0 else 1
    per = 8
    groups = [kv_refs[i : i + per] for i in range(0, len(kv_refs), per)]

    def slot(s, carry):
        steps = [(h, i) for h in range(heads // pair) for i in range(len(groups))]

        def rows(h):
            parts = [q_ref[0, :, (h * pair + j) * 128 : (h * pair + j + 1) * 128] for j in range(pair)]
            return jnp.concatenate(parts, axis=0)

        def part(i, low):
            return jnp.concatenate([ref[first + s, :, low : low + 128] for ref, first in groups[i]], axis=0)

        def score(step):
            h, i = step
            return lax.dot_general(rows(h), part(i, 0), NT, preferred_element_type=F32)

        now = score(steps[0])
        total = None
        sums = sum_ref[0]
        lane = lane_of(tok)
        for at, (h, i) in enumerate(steps):
            later = score(steps[at + 1]) if at + 1 < len(steps) else None
            probs = jnp.exp2(now * scale).astype(BF16)
            values = part(i, 128)
            both = jnp.concatenate([values, jnp.ones_like(values)], axis=1)
            update = jnp.dot(probs, both, preferred_element_type=F32)
            total = update if i == 0 else total + update
            if i == len(groups) - 1:
                for j in range(pair):
                    head = h * pair + j
                    mine = total[j * tok : (j + 1) * tok]
                    acc_ref[0, :, head * 128 : (head + 1) * 128] += mine[:, :128]
                    sums = jnp.where(lane == head, sums + mine[:, 128:], sums)
            now = later
        sum_ref[0] = sums
        return carry

    lax.fori_loop(0, count, slot, 0)


def first_kernel(kv_first, scale, count_ref, q_ref, *refs):
    kv, (acc_ref, sum_ref) = refs[:-2], refs[-2:]
    acc_ref[...] = jnp.zeros_like(acc_ref)
    sum_ref[...] = jnp.zeros_like(sum_ref)
    add_blocks(count_ref[0], q_ref, [(kv[i], b) for i, b in kv_first], acc_ref, sum_ref, scale)


def next_kernel(kv_first, scale, count_ref, q_ref, acc_in, sum_in, *refs):
    kv, (acc_ref, sum_ref) = refs[:-2], refs[-2:]
    acc_ref[...] = acc_in[...]
    sum_ref[...] = sum_in[...]
    add_blocks(count_ref[0], q_ref, [(kv[i], b) for i, b in kv_first], acc_ref, sum_ref, scale)


def slow_rows(count, q_ref, blocks, acc_ref, sum_ref, top_ref, held, scale):
    tok = q_ref.shape[1]
    heads = q_ref.shape[2] // 128
    lane = lane_of(tok)
    acc_ref[...] = jnp.zeros_like(acc_ref)
    sum_ref[...] = jnp.zeros_like(sum_ref)
    top_ref[...] = jnp.full_like(top_ref, -1e30)

    def one(b, carry):
        for i, (ref, first) in enumerate(blocks):

            @pl.when(b % len(blocks) == i)
            def _():
                pltpu.sync_copy(ref.at[first + b // len(blocks)], held)

        keys = held[:, :128]
        values = held[:, 128:]
        tops = top_ref[...]
        sums = sum_ref[0]
        for h in range(heads):
            cols = slice(h * 128, (h + 1) * 128)
            scores = lax.dot_general(q_ref[0, :, cols], keys, NT, preferred_element_type=F32) * scale
            old = jnp.max(jnp.where(lane == h, tops, -jnp.inf), axis=1, keepdims=True)
            new = jnp.maximum(old, jnp.max(scores, axis=1, keepdims=True))
            back = jnp.exp2(old - new)
            probs = jnp.exp2(scores - new)
            update = jnp.dot(probs.astype(BF16), values, preferred_element_type=F32)
            acc_ref[0, :, cols] = acc_ref[0, :, cols] * back + update
            sums = jnp.where(lane == h, sums * back + jnp.sum(probs, axis=1, keepdims=True), sums)
            tops = jnp.where(lane == h, new, tops)
        top_ref[...] = tops
        sum_ref[0] = sums
        return carry

    lax.fori_loop(0, count * len(blocks), one, 0)


def last_kernel(kv_first, all_first, n_kv, scale, count_ref, q_ref, acc_in, sum_in, *refs):
    kv = refs[:n_kv]
    every = refs[n_kv:-5]
    out_ref, acc_ref, sum_ref, top_ref, held = refs[-5:]
    tok = q_ref.shape[1]
    heads = q_ref.shape[2] // 128
    lane = lane_of(tok)
    count = count_ref[0]
    acc_ref[...] = acc_in[...]
    sum_ref[...] = sum_in[...]
    top_ref[...] = jnp.zeros_like(top_ref)
    add_blocks(count, q_ref, [(kv[i], b) for i, b in kv_first], acc_ref, sum_ref, scale)
    sums = sum_ref[0]
    good = (sums > SUM_LOW) & (sums < SUM_HIGH)
    bad = jnp.max(jnp.where((lane < heads) & jnp.logical_not(good), 1.0, 0.0))

    @pl.when(bad > 0.0)
    def _():
        slow_rows(count, q_ref, [(every[i], b) for i, b in all_first], acc_ref, sum_ref, top_ref, held, scale)

    sums = jnp.where(lane < heads, sum_ref[0], 1.0)
    weight = jnp.log(sums) * (1.0 / math.log(2.0)) + top_ref[...]
    inverse = 1.0 / sums
    for h in range(heads):
        cols = slice(h * 128, (h + 1) * 128)
        by = jnp.sum(jnp.where(lane == h, inverse, 0.0), axis=1, keepdims=True)
        out_ref[0, :, cols] = (acc_ref[0, :, cols] * by).astype(BF16)
    first = weight.astype(BF16).astype(F32)
    second = (weight - first).astype(BF16).astype(F32)
    third = weight - first - second
    packed = jnp.where(lane < 8, first, 0.0)
    packed = packed + pltpu.roll(jnp.where(lane < 8, second, 0.0), 8, 1)
    packed = packed + pltpu.roll(jnp.where(lane < 8, third, 0.0), 16, 1)
    out_ref[0, :, heads * 128 :] = packed.astype(BF16)


def merge_kernel(n, *refs):
    parts, gate_ref, out_ref = refs[:n], refs[n], refs[n + 1]
    tok = out_ref.shape[1]
    heads = out_ref.shape[2] // 128
    lane = lane_of(tok)
    weights = []
    for ref in parts:
        packed = ref[0, :, heads * 128 :].astype(F32)
        weights.append(packed + pltpu.roll(packed, 120, 1) + pltpu.roll(packed, 112, 1))
    top = functools.reduce(jnp.maximum, weights)
    weights = [jnp.exp2(w - top) for w in weights]
    inverse = 1.0 / functools.reduce(jnp.add, weights)
    weights = [w * inverse for w in weights]
    mixed = []
    square = jnp.zeros((tok, 128), F32)
    for h in range(heads):
        cols = slice(h * 128, (h + 1) * 128)
        value = None
        for ref, w in zip(parts, weights):
            by = jnp.sum(jnp.where(lane == h, w, 0.0), axis=1, keepdims=True)
            term = ref[0, :, cols].astype(F32) * by
            value = term if value is None else value + term
        mixed.append(value)
        square = square + value * value
    mean = jnp.sum(square, axis=1, keepdims=True) * (1.0 / (heads * 128))
    factor = lax.rsqrt(mean + 1e-06)
    for h in range(heads):
        cols = slice(h * 128, (h + 1) * 128)
        out_ref[0, :, cols] = (gate_ref[:, cols] * (mixed[h] * factor)).astype(BF16)


def whole(shape):
    return pl.BlockSpec(shape, lambda g: (0,) * len(shape))


def pieces_of(arrays, n):
    return [(i, f) for i, a in enumerate(arrays) for f in range(0, a.shape[0], n)]


def attend(n, count, queries, groups, arrays, state, every=None):
    tok, width = queries.shape[1:]
    start = groups[0]
    size = len(groups)
    scale = 128 ** (-0.5) * math.log2(math.e)
    here = lambda g: (start + g, 0, 0)
    plain = lambda g: (g, 0, 0)
    smem = pl.BlockSpec(memory_space=pltpu.SMEM)
    kv_specs = [whole(a.shape) for a in arrays]
    first = pieces_of(arrays, n)
    keys = n * 128 * len(first)
    cost = pl.CostEstimate(
        flops=4 * size * tok * width * keys,
        bytes_accessed=size * tok * width * 12,
        transcendentals=size * tok * (width // 128) * keys,
    )
    params = pltpu.CompilerParams(vmem_limit_bytes=VMEM)
    state_specs = [pl.BlockSpec((1, tok, width), here), pl.BlockSpec((1, tok, 128), here)]
    out_state = [jax.ShapeDtypeStruct((size, tok, width), F32), jax.ShapeDtypeStruct((size, tok, 128), F32)]
    out_specs = [pl.BlockSpec((1, tok, width), plain), pl.BlockSpec((1, tok, 128), plain)]
    q_spec = pl.BlockSpec((1, tok, width), here)
    if every is None:
        body = first_kernel if state is None else next_kernel
        given = [] if state is None else list(state)
        return pl.pallas_call(
            functools.partial(body, first, scale),
            grid=(size,),
            in_specs=[smem, q_spec] + (state_specs if given else []) + kv_specs,
            out_specs=out_specs,
            out_shape=out_state,
            compiler_params=params,
            cost_estimate=cost,
        )(count, queries, *given, *arrays)
    return pl.pallas_call(
        functools.partial(last_kernel, first, pieces_of(every, n), len(arrays), scale),
        grid=(size,),
        in_specs=[smem, q_spec] + state_specs + kv_specs + [pl.BlockSpec(memory_space=pl.ANY)] * len(every),
        out_specs=pl.BlockSpec((1, tok, width + 128), plain),
        out_shape=jax.ShapeDtypeStruct((size, tok, width + 128), BF16),
        scratch_shapes=[
            pltpu.VMEM((1, tok, width), F32),
            pltpu.VMEM((1, tok, 128), F32),
            pltpu.VMEM((tok, 128), F32),
            pltpu.VMEM((tok, 256), BF16),
        ],
        compiler_params=params,
        cost_estimate=cost,
    )(count, queries, *state, *arrays, *every)


def merge(parts, gate):
    tok, width = parts[0].shape[1], gate.shape[1]
    return pl.pallas_call(
        functools.partial(merge_kernel, len(parts)),
        out_shape=jax.ShapeDtypeStruct((1, tok, width), BF16),
        compiler_params=pltpu.CompilerParams(vmem_limit_bytes=VMEM),
    )(*parts, gate)


def shift(value, axis, by):
    size = lax.axis_size(axis)
    return lax.ppermute(value, axis, [(i, (i + by) % size) for i in range(size)])


def upward(value, by):
    size = lax.axis_size("span")
    return lax.ppermute(value, "span", [(i, i + by) for i in range(size - by)])


def shards(query, key, value, noise_step, span_mask, gate_weight):
    here = lax.axis_index("span")
    mask_row = lax.dynamic_slice_in_dim(span_mask, here, 1, 0)[0]
    step_now = lax.dynamic_slice_in_dim(noise_step, here, 1, 0)
    own = jnp.concatenate([key, value], axis=2)
    queries = jnp.concatenate([query, shift(query, "x", 2), shift(query, "x", 1), shift(query, "x", -1)], axis=0)
    below = [upward(own, by) for by in (1, 2, 3)]
    may = [(here >= by) & (mask_row[jnp.maximum(here - by, 0)] > 0) for by in (1, 2, 3)]
    second = jnp.where(may[0], below[0], jnp.where(may[1], below[1], below[2]))
    third = jnp.where(may[0] & may[1], below[1], below[2])
    count = 1 + sum(m.astype(jnp.int32) for m in may)
    gate = noise_gate(step_now, gate_weight, gate_weight.shape[0])
    n = 4
    slots = jnp.concatenate([own, second, third, below[2]], axis=0)
    count = count.reshape(1)
    a0 = jnp.concatenate([slots, shift(slots, "zl", 1)], axis=0)
    a1, a2 = shift(a0, "y", 1), shift(a0, "y", -1)
    b0 = shift(a0, "core", 1)
    b1, b2 = shift(a1, "core", 1), shift(a2, "core", 1)
    a3 = jnp.concatenate([shift(a1[:n], "y", 1), shift(a2[n:], "y", -1)], axis=0)
    b3 = shift(a3, "core", 1)
    every = [a0, b0, a1, b1, a2, b2, a3, b3]
    state = attend(n, count, queries, [0, 1, 2, 3], every[:2], None)
    state = attend(n, count, queries, [0, 1, 2, 3], every[2:6], state)
    far = attend(n, count, queries, [1], every[6:], state, every)
    far = shift(far, "x", 2)
    left = attend(n, count, queries, [2], every[6:], state, every)
    left = shift(left, "x", -1)
    right = attend(n, count, queries, [3], every[6:], state, every)
    right = shift(right, "x", 1)
    mine = attend(n, count, queries, [0], every[6:], state, every)
    return merge([mine, far, left, right], gate)


def solution(mesh):
    fine = Mesh(mesh.devices.reshape(4, 4, 4, 2, 2), ("span", "x", "y", "zl", "core"))
    rows = P("span", ("x", "y", "zl", "core"), None)
    return jax.shard_map(
        shards,
        mesh=fine,
        in_specs=(rows, rows, rows, P(), P(), P()),
        out_specs=rows,
        check_vma=False,
    )
```

```python
import functools
import itertools
import math

import jax
import jax.numpy as jnp
from jax import lax
from jax.experimental import pallas as pl
from jax.experimental.pallas import tpu as pltpu
from jax.sharding import Mesh, PartitionSpec as P

STEPS = 64
NT = (((1,), (1,)), ((), ()))
F32 = jnp.float32
BF16 = jnp.bfloat16
SUM_LOW = 2.0**-80
SUM_HIGH = 2.0**100
VMEM = 24 << 20


def noise_gate(step_now, gate_weight, embed_width):
    half = embed_width // 2
    freqs = jnp.exp(-math.log(10000.0) * jnp.arange(half, dtype=F32) / half)
    angles = step_now.astype(F32)[:, None] * (1000.0 / STEPS) * freqs[None, :]
    embed = jnp.concatenate([jnp.cos(angles), jnp.sin(angles)], axis=1)
    return jax.nn.sigmoid(jnp.dot(embed, gate_weight, precision=lax.Precision.HIGHEST))


def lane_of(rows):
    return lax.broadcasted_iota(jnp.int32, (rows, 128), 1)


def add_blocks(count, q_ref, blocks, acc_ref, stat_ref, scale):
    tok = q_ref.shape[1]
    heads = q_ref.shape[2] // 128
    pair = 2 if heads % 2 == 0 else 1
    groups = [blocks[i : i + 8] for i in range(0, len(blocks), 8)]
    steps = [(g, h, i) for g in range(q_ref.shape[0]) for h in range(heads // pair) for i in range(len(groups))]
    lane = lane_of(tok)

    def rows(g, h):
        parts = [q_ref[g, :, (h * pair + j) * 128 : (h * pair + j + 1) * 128] for j in range(pair)]
        return jnp.concatenate(parts, axis=0)

    def slot(s, carry):
        def part(i, low):
            return jnp.concatenate([ref[first + s, :, low : low + 128] for ref, first in groups[i]], axis=0)

        def score(step):
            g, h, i = step
            return lax.dot_general(rows(g, h), part(i, 0), NT, preferred_element_type=F32)

        now = score(steps[0])
        total = None
        for at, (g, h, i) in enumerate(steps):
            later = score(steps[at + 1]) if at + 1 < len(steps) else None
            probs = jnp.exp2(now * scale).astype(BF16)
            values = part(i, 128)
            both = jnp.concatenate([values, jnp.ones_like(values)], axis=1)
            update = jnp.dot(probs, both, preferred_element_type=F32)
            total = update if i == 0 else total + update
            if i == len(groups) - 1:
                for j in range(pair):
                    head = h * pair + j
                    mine = total[j * tok : (j + 1) * tok]
                    acc_ref[g, :, head * 128 : (head + 1) * 128] += mine[:, :128]
                    stat_ref[g, :, :128] = jnp.where(lane == head, stat_ref[g, :, :128] + mine[:, 128:], stat_ref[g, :, :128])
            now = later
        return carry

    lax.fori_loop(0, count, slot, 0)


def add_blocks_slow(count, q_ref, blocks, acc_ref, stat_ref, block_ref, scale, g):
    tok = q_ref.shape[1]
    heads = q_ref.shape[2] // 128
    lane = lane_of(tok)

    def head(h, carry):
        cols = pl.ds(pl.multiple_of(h * 128, 128), 128)
        scores = lax.dot_general(q_ref[g, :, cols], block_ref[:, :128], NT, preferred_element_type=F32) * scale
        sums = stat_ref[g, :, :128]
        tops = stat_ref[g, :, 128:]
        old = jnp.max(jnp.where(lane == h, tops, -jnp.inf), axis=1, keepdims=True)
        new = jnp.maximum(old, jnp.max(scores, axis=1, keepdims=True))
        back = jnp.exp2(old - new)
        probs = jnp.exp2(scores - new)
        update = jnp.dot(probs.astype(BF16), block_ref[:, 128:], preferred_element_type=F32)
        acc_ref[g, :, cols] = acc_ref[g, :, cols] * back + update
        total = sums * back + jnp.sum(probs, axis=1, keepdims=True)
        stat_ref[g, :, :128] = jnp.where(lane == h, total, sums)
        stat_ref[g, :, 128:] = jnp.where(lane == h, new, tops)
        return carry

    def one(b, carry):
        for i, (ref, first) in enumerate(blocks):

            @pl.when(lax.rem(b, len(blocks)) == i)
            def _(ref=ref, first=first):
                block_ref[...] = ref[first + lax.div(b, len(blocks))]

        lax.fori_loop(0, heads, head, 0)
        return carry

    lax.fori_loop(0, count * len(blocks), one, 0)


def attend_kernel(runs, start, begin, finish, scale, count_ref, *refs):
    refs = list(refs)
    block_ref = refs.pop()
    flag_in = None if begin else refs.pop(0)
    q_ref = refs.pop(0)
    acc_in, stat_in = (None, None) if begin else (refs.pop(0), refs.pop(0))
    out_ref = None
    if finish:
        out_ref, acc_ref, stat_ref = refs[-3:]
    else:
        acc_ref, stat_ref, flag_out = refs[-3:]
    blocks = [(refs[i], first) for i, first in runs]
    size, tok = q_ref.shape[:2]
    heads = q_ref.shape[2] // 128
    lane = lane_of(tok)
    count = count_ref[0]
    step = pl.program_id(0) * size
    if begin:
        acc_ref[...] = jnp.zeros_like(acc_ref)
        stat_ref[...] = jnp.zeros_like(stat_ref)
    else:
        acc_ref[...] = acc_in[...]
        stat_ref[...] = stat_in[...]
    add_blocks(count, q_ref, blocks, acc_ref, stat_ref, scale)
    sums = [stat_ref[g, :, :128] for g in range(size)]
    low = functools.reduce(jnp.minimum, sums)
    high = functools.reduce(jnp.maximum, sums)
    good = (low > SUM_LOW) & (high < SUM_HIGH)
    slow = jnp.max(jnp.where((lane < heads) & jnp.logical_not(good), 1.0, 0.0)) > 0.0
    if not begin:
        for g in range(size):
            slow = slow | (flag_in[start + step + g] > 0)

    @pl.when(slow)
    def _():
        def group(g, carry):
            if begin:
                acc_ref[g] = jnp.zeros(acc_ref.shape[1:], F32)
                stat_ref[g, :, :128] = jnp.zeros((tok, 128), F32)
                stat_ref[g, :, 128:] = jnp.full((tok, 128), -1e30, F32)
            else:
                acc_ref[g] = acc_in[g]
                stat_ref[g] = stat_in[g]
            add_blocks_slow(count, q_ref, blocks, acc_ref, stat_ref, block_ref, scale, g)
            return carry

        lax.fori_loop(0, size, group, 0)

    if not finish:
        for g in range(size):
            flag_out[step + g] = jnp.where(slow, 1, 0)
        return
    for g in range(size):
        pack(acc_ref, stat_ref, out_ref, g)


def pack(acc_ref, stat_ref, out_ref, g):
    tok = out_ref.shape[1]
    heads = out_ref.shape[2] // 128 - 1
    lane = lane_of(tok)
    sums = jnp.where(lane < heads, stat_ref[g, :, :128], 1.0)
    weight = jnp.log(sums) * (1.0 / math.log(2.0)) + stat_ref[g, :, 128:]
    inverse = 1.0 / sums
    for h in range(heads):
        cols = slice(h * 128, (h + 1) * 128)
        out_ref[g, :, cols] = (acc_ref[g, :, cols] * inverse[:, h : h + 1]).astype(BF16)
    first = weight.astype(BF16).astype(F32)
    second = (weight - first).astype(BF16).astype(F32)
    third = weight - first - second
    packed = jnp.where(lane < 8, first, 0.0)
    packed = packed + pltpu.roll(jnp.where(lane < 8, second, 0.0), 8, 1)
    packed = packed + pltpu.roll(jnp.where(lane < 8, third, 0.0), 16, 1)
    out_ref[g, :, heads * 128 :] = packed.astype(BF16)


def merge_kernel(n, *refs):
    parts, gate_ref, out_ref = refs[:n], refs[n], refs[n + 1]
    tok = out_ref.shape[1]
    heads = out_ref.shape[2] // 128
    weights = []
    for ref in parts:
        packed = ref[0, :, heads * 128 :].astype(F32)
        weights.append(packed + pltpu.roll(packed, 120, 1) + pltpu.roll(packed, 112, 1))
    top = functools.reduce(jnp.maximum, weights)
    weights = [jnp.exp2(w - top) for w in weights]
    inverse = 1.0 / functools.reduce(jnp.add, weights)
    weights = [w * inverse for w in weights]
    mixed = []
    square = jnp.zeros((tok, 128), F32)
    for h in range(heads):
        cols = slice(h * 128, (h + 1) * 128)
        value = None
        for ref, w in zip(parts, weights):
            term = ref[0, :, cols].astype(F32) * w[:, h : h + 1]
            value = term if value is None else value + term
        mixed.append(value)
        square = square + value * value
    mean = jnp.sum(square, axis=1, keepdims=True) * (1.0 / (heads * 128))
    factor = lax.rsqrt(mean + 1e-06)
    for h in range(heads):
        cols = slice(h * 128, (h + 1) * 128)
        out_ref[0, :, cols] = (gate_ref[:, cols] * (mixed[h] * factor)).astype(BF16)


def whole(shape):
    return pl.BlockSpec(shape, lambda g: (0,) * len(shape))


def runs_of(arrays, n):
    return [(i, f) for i, a in enumerate(arrays) for f in range(0, a.shape[0], n)]


def attend(n, count, queries, start, size, arrays, state, finish, batch=1):
    tok, width = queries.shape[1:]
    scale = 128 ** (-0.5) * math.log2(math.e)
    here = lambda g: (start // batch + g, 0, 0)
    plain = lambda g: (g, 0, 0)
    smem = pl.BlockSpec(memory_space=pltpu.SMEM)
    runs = runs_of(arrays, n)
    keys = n * 128 * len(runs)
    begin = state is None
    given, given_specs = [], []
    if not begin:
        given = list(state[:2])
        given_specs = [pl.BlockSpec((batch, tok, width), here), pl.BlockSpec((batch, tok, 256), here)]
    if finish:
        outs = jax.ShapeDtypeStruct((size, tok, width + 128), BF16)
        out_specs = pl.BlockSpec((batch, tok, width + 128), plain)
        scratch = [pltpu.VMEM((batch, tok, width), F32), pltpu.VMEM((batch, tok, 256), F32)]
    else:
        outs = [
            jax.ShapeDtypeStruct((size, tok, width), F32),
            jax.ShapeDtypeStruct((size, tok, 256), F32),
            jax.ShapeDtypeStruct((size,), jnp.int32),
        ]
        out_specs = [pl.BlockSpec((batch, tok, width), plain), pl.BlockSpec((batch, tok, 256), plain), smem]
        scratch = []
    return pl.pallas_call(
        functools.partial(attend_kernel, runs, start, begin, finish, scale),
        grid=(size // batch,),
        in_specs=[smem]
        + ([] if begin else [smem])
        + [pl.BlockSpec((batch, tok, width), here)]
        + given_specs
        + [whole(a.shape) for a in arrays],
        out_specs=out_specs,
        out_shape=outs,
        scratch_shapes=scratch + [pltpu.VMEM((tok, 256), BF16)],
        compiler_params=pltpu.CompilerParams(vmem_limit_bytes=VMEM),
        cost_estimate=pl.CostEstimate(
            flops=4 * size * tok * width * keys,
            bytes_accessed=size * tok * width * 12,
            transcendentals=size * tok * (width // 128) * keys,
        ),
    )(count, *([] if begin else [state[2]]), queries, *given, *arrays)


def merge(parts, gate):
    tok, width = parts[0].shape[1], gate.shape[1]
    return pl.pallas_call(
        functools.partial(merge_kernel, len(parts)),
        out_shape=jax.ShapeDtypeStruct((1, tok, width), BF16),
        compiler_params=pltpu.CompilerParams(vmem_limit_bytes=VMEM),
    )(*parts, gate)


def shift(value, axis, by):
    size = lax.axis_size(axis)
    return lax.ppermute(value, axis, [(i, (i + by) % size) for i in range(size)])


def upward(value, by):
    size = lax.axis_size("span")
    return lax.ppermute(value, "span", [(i, i + by) for i in range(size - by)])


def partner(value, axes):
    sizes = [lax.axis_size(axis) for axis in axes]
    pairs = []
    for place in itertools.product(*[range(size) for size in sizes]):
        to = [at ^ 1 for at in place]
        pairs.append(tuple(functools.reduce(lambda i, part: i * part[1] + part[0], zip(p, sizes), 0) for p in (place, to)))
    return lax.ppermute(value, axes, pairs)


def mirror(value, axis):
    size = lax.axis_size(axis)
    return lax.ppermute(value, axis, [(i, size - 1 - i) for i in range(size)])


def shards(query, key, value, noise_step, span_mask, gate_weight):
    tie = lax.optimization_barrier
    here = lax.axis_index("span")
    mask_row = lax.dynamic_slice_in_dim(span_mask, here, 1, 0)[0]
    step_now = lax.dynamic_slice_in_dim(noise_step, here, 1, 0)
    own = jnp.concatenate([key, value], axis=2)
    own, query = tie((own, query))
    below = [upward(own, by) for by in (1, 2, 3)]
    beside = partner(query, ("x",))
    below, beside = tie((below, beside))
    may = [(here >= by) & (mask_row[jnp.maximum(here - by, 0)] > 0) for by in (1, 2, 3)]
    count = (1 + sum(m.astype(jnp.int32) for m in may)).reshape(1)
    second = jnp.where(may[0], below[0], jnp.where(may[1], below[1], below[2]))
    third = jnp.where(may[0] & may[1], below[1], below[2])
    slots = jnp.concatenate([own, second, third, below[2]], axis=0)
    n = slots.shape[0]
    a0 = jnp.concatenate([slots, mirror(slots, "x")], axis=0)
    held = jnp.concatenate([beside, query], axis=0)
    queries = jnp.concatenate([partner(held, ("zl",)), held], axis=0)
    gate = noise_gate(step_now, gate_weight, gate_weight.shape[0])
    a0, queries, gate, count = tie((a0, queries, gate, count))
    a1, a2 = shift(a0, "y", 1), shift(a0, "y", -1)
    b0 = shift(a0, "core", 1)
    state = attend(n, count, queries, 0, 4, [a0, b0], None, False, 4)
    a1, a2, state = tie((a1, a2, state))
    a3 = [shift(a1[:n], "y", 1), shift(a2[n:], "y", -1)]
    b1, b2 = shift(a1, "core", 1), shift(a2, "core", 1)
    rest = attend(n, count, queries, 0, 3, [a1, a2, b1, b2], state, False, 3)
    a3, rest = tie((a3, rest))
    a3 = jnp.concatenate(a3, axis=0)
    b3 = shift(a3, "core", 1)
    rest = attend(n, count, queries, 0, 3, [a3, b3], rest, True, 3)
    state, a3, b3, rest = tie((state, a3, b3, rest))
    opposite = partner(rest[0:1], ("x", "zl"))
    sides = [partner(rest[1:2], ("zl",)), partner(rest[2:3], ("x",))]
    near = attend(n, count, queries, 3, 1, [a1, a2, b1, b2, a3, b3], state, True)
    opposite, sides, near = tie((opposite, sides, near))
    return merge([near, opposite, *sides], gate)


def solution(mesh):
    fine = Mesh(mesh.devices.reshape(4, 4, 4, 2, 2), ("span", "x", "y", "zl", "core"))
    rows = P("span", ("x", "y", "zl", "core"), None)
    return jax.shard_map(
        shards,
        mesh=fine,
        in_specs=(rows, rows, rows, P(), P(), P()),
        out_specs=rows,
        check_vma=False,
    )
```

```python
import functools
import itertools
import math

import jax
import jax.numpy as jnp
from jax import lax
from jax.experimental import pallas as pl
from jax.experimental.pallas import tpu as pltpu
from jax.sharding import Mesh, PartitionSpec as P

STEPS = 64
NT = (((1,), (1,)), ((), ()))
F32 = jnp.float32
BF16 = jnp.bfloat16
SUM_LOW = 2.0**-80
SUM_HIGH = 2.0**100
VMEM = 24 << 20


def noise_gate(step_now, gate_weight, embed_width):
    half = embed_width // 2
    freqs = jnp.exp(-math.log(10000.0) * jnp.arange(half, dtype=F32) / half)
    angles = step_now.astype(F32)[:, None] * (1000.0 / STEPS) * freqs[None, :]
    embed = jnp.concatenate([jnp.cos(angles), jnp.sin(angles)], axis=1)
    return jax.nn.sigmoid(jnp.dot(embed, gate_weight, precision=lax.Precision.HIGHEST))


def lane_of(rows):
    return lax.broadcasted_iota(jnp.int32, (rows, 128), 1)


def allowed_spans(mask_ref):
    here = lax.axis_index("span")
    may = [jnp.where(mask_ref[here, here ^ by] > 0, 1, 0) for by in (1, 2, 3)]

    def place(j):
        first = jnp.where(may[0] > 0, 0, jnp.where(may[1] > 0, 1, 2))
        second = jnp.where(may[0] * may[1] > 0, 1, 2)
        return jnp.where(j == 0, first, jnp.where(j == 1, second, 2))

    return may[0] + may[1] + may[2], place


def add_blocks(count, pick, q_ref, blocks, acc_ref, stat_ref, scale):
    tok = q_ref.shape[1]
    heads = q_ref.shape[2] // 128
    pair = 2 if heads % 2 == 0 else 1
    groups = [blocks[i : i + 8] for i in range(0, len(blocks), 8)]
    steps = [(g, h, i) for g in range(q_ref.shape[0]) for h in range(heads // pair) for i in range(len(groups))]
    lane = lane_of(tok)

    def rows(g, h):
        parts = [q_ref[g, :, (h * pair + j) * 128 : (h * pair + j + 1) * 128] for j in range(pair)]
        return jnp.concatenate(parts, axis=0)

    def slot(s, carry):
        s = pick(s)

        def part(i, low):
            return jnp.concatenate([ref[first + s, :, low : low + 128] for ref, first in groups[i]], axis=0)

        def score(step):
            g, h, i = step
            return lax.dot_general(rows(g, h), part(i, 0), NT, preferred_element_type=F32)

        now = score(steps[0])
        total = None
        for at, (g, h, i) in enumerate(steps):
            later = score(steps[at + 1]) if at + 1 < len(steps) else None
            probs = jnp.exp2(now * scale).astype(BF16)
            values = part(i, 128)
            both = jnp.concatenate([values, jnp.ones_like(values)], axis=1)
            update = jnp.dot(probs, both, preferred_element_type=F32)
            total = update if i == 0 else total + update
            if i == len(groups) - 1:
                for j in range(pair):
                    head = h * pair + j
                    mine = total[j * tok : (j + 1) * tok]
                    acc_ref[g, :, head * 128 : (head + 1) * 128] += mine[:, :128]
                    stat_ref[g, :, :128] = jnp.where(lane == head, stat_ref[g, :, :128] + mine[:, 128:], stat_ref[g, :, :128])
            now = later
        return carry

    lax.fori_loop(0, count, slot, 0)


def add_blocks_slow(count, pick, q_ref, blocks, acc_ref, stat_ref, block_ref, scale, g):
    tok = q_ref.shape[1]
    heads = q_ref.shape[2] // 128
    lane = lane_of(tok)

    def head(h, carry):
        cols = pl.ds(pl.multiple_of(h * 128, 128), 128)
        scores = lax.dot_general(q_ref[g, :, cols], block_ref[:, :128], NT, preferred_element_type=F32) * scale
        sums = stat_ref[g, :, :128]
        tops = stat_ref[g, :, 128:]
        old = jnp.max(jnp.where(lane == h, tops, -jnp.inf), axis=1, keepdims=True)
        new = jnp.maximum(old, jnp.max(scores, axis=1, keepdims=True))
        back = jnp.exp2(old - new)
        probs = jnp.exp2(scores - new)
        update = jnp.dot(probs.astype(BF16), block_ref[:, 128:], preferred_element_type=F32)
        acc_ref[g, :, cols] = acc_ref[g, :, cols] * back + update
        total = sums * back + jnp.sum(probs, axis=1, keepdims=True)
        stat_ref[g, :, :128] = jnp.where(lane == h, total, sums)
        stat_ref[g, :, 128:] = jnp.where(lane == h, new, tops)
        return carry

    def one(b, carry):
        for i, (ref, first) in enumerate(blocks):

            @pl.when(lax.rem(b, len(blocks)) == i)
            def _(ref=ref, first=first):
                block_ref[...] = ref[first + pick(lax.div(b, len(blocks)))]

        lax.fori_loop(0, heads, head, 0)
        return carry

    lax.fori_loop(0, count * len(blocks), one, 0)


def attend_kernel(parts, start, begin, finish, scale, mask_ref, *refs):
    refs = list(refs)
    block_ref = refs.pop()
    flag_in = None if begin else refs.pop(0)
    q_ref = refs.pop(0)
    acc_in, stat_in = (None, None) if begin else (refs.pop(0), refs.pop(0))
    out_ref = None
    if finish:
        out_ref, acc_ref, stat_ref = refs[-3:]
    else:
        acc_ref, stat_ref, flag_out = refs[-3:]
    others, place = allowed_spans(mask_ref)
    todo = []
    for runs, lead in parts:
        pick = lambda s, lead=lead: jnp.where(s < lead, s, lead + place(s - lead))
        todo.append(([(refs[i], first) for i, first in runs], lead + others, pick))
    size, tok = q_ref.shape[:2]
    heads = q_ref.shape[2] // 128
    lane = lane_of(tok)
    step = pl.program_id(0) * size
    if begin:
        acc_ref[...] = jnp.zeros_like(acc_ref)
        stat_ref[...] = jnp.zeros_like(stat_ref)
    else:
        acc_ref[...] = acc_in[...]
        stat_ref[...] = stat_in[...]
    for blocks, count, pick in todo:
        add_blocks(count, pick, q_ref, blocks, acc_ref, stat_ref, scale)
    sums = [stat_ref[g, :, :128] for g in range(size)]
    low = functools.reduce(jnp.minimum, sums)
    high = functools.reduce(jnp.maximum, sums)
    good = (low > SUM_LOW) & (high < SUM_HIGH)
    slow = jnp.max(jnp.where((lane < heads) & jnp.logical_not(good), 1.0, 0.0)) > 0.0
    if not begin:
        for g in range(size):
            slow = slow | (flag_in[start + step + g] > 0)

    @pl.when(slow)
    def _():
        def group(g, carry):
            if begin:
                acc_ref[g] = jnp.zeros(acc_ref.shape[1:], F32)
                stat_ref[g, :, :128] = jnp.zeros((tok, 128), F32)
                stat_ref[g, :, 128:] = jnp.full((tok, 128), -1e30, F32)
            else:
                acc_ref[g] = acc_in[g]
                stat_ref[g] = stat_in[g]
            for blocks, count, pick in todo:
                add_blocks_slow(count, pick, q_ref, blocks, acc_ref, stat_ref, block_ref, scale, g)
            return carry

        lax.fori_loop(0, size, group, 0)

    if not finish:
        for g in range(size):
            flag_out[step + g] = jnp.where(slow, 1, 0)
        return
    for g in range(size):
        pack(acc_ref, stat_ref, out_ref, g)


def pack(acc_ref, stat_ref, out_ref, g):
    tok = out_ref.shape[1]
    heads = out_ref.shape[2] // 128 - 1
    lane = lane_of(tok)
    sums = jnp.where(lane < heads, stat_ref[g, :, :128], 1.0)
    weight = jnp.log(sums) * (1.0 / math.log(2.0)) + stat_ref[g, :, 128:]
    inverse = 1.0 / sums
    for h in range(heads):
        cols = slice(h * 128, (h + 1) * 128)
        out_ref[g, :, cols] = (acc_ref[g, :, cols] * inverse[:, h : h + 1]).astype(BF16)
    first = weight.astype(BF16).astype(F32)
    second = (weight - first).astype(BF16).astype(F32)
    third = weight - first - second
    packed = jnp.where(lane < 8, first, 0.0)
    packed = packed + pltpu.roll(jnp.where(lane < 8, second, 0.0), 8, 1)
    packed = packed + pltpu.roll(jnp.where(lane < 8, third, 0.0), 16, 1)
    out_ref[g, :, heads * 128 :] = packed.astype(BF16)


def merge_kernel(n, *refs):
    parts, gate_ref, out_ref = refs[:n], refs[n], refs[n + 1]
    tok = out_ref.shape[1]
    heads = out_ref.shape[2] // 128
    rows = lax.broadcasted_iota(jnp.int32, gate_ref.shape, 0)
    mine = jnp.where(rows == lax.axis_index("span"), gate_ref[...], 0.0)
    gate = jnp.sum(mine, axis=0, keepdims=True)
    weights = []
    for ref in parts:
        packed = ref[0, :, heads * 128 :].astype(F32)
        weights.append(packed + pltpu.roll(packed, 120, 1) + pltpu.roll(packed, 112, 1))
    top = functools.reduce(jnp.maximum, weights)
    weights = [jnp.exp2(w - top) for w in weights]
    inverse = 1.0 / functools.reduce(jnp.add, weights)
    weights = [w * inverse for w in weights]
    mixed = []
    square = jnp.zeros((tok, 128), F32)
    for h in range(heads):
        cols = slice(h * 128, (h + 1) * 128)
        value = None
        for ref, w in zip(parts, weights):
            term = ref[0, :, cols].astype(F32) * w[:, h : h + 1]
            value = term if value is None else value + term
        mixed.append(value)
        square = square + value * value
    mean = jnp.sum(square, axis=1, keepdims=True) * (1.0 / (heads * 128))
    factor = lax.rsqrt(mean + 1e-06)
    for h in range(heads):
        cols = slice(h * 128, (h + 1) * 128)
        out_ref[0, :, cols] = (gate[:, cols] * (mixed[h] * factor)).astype(BF16)


def whole(shape):
    return pl.BlockSpec(shape, lambda g: (0,) * len(shape))


def runs_of(arrays, n, at):
    return [(at + i, f) for i, a in enumerate(arrays) for f in range(0, a.shape[0], n)]


def attend(mask, queries, start, size, pieces, state, finish, batch=1):
    tok, width = queries.shape[1:]
    scale = 128 ** (-0.5) * math.log2(math.e)
    here = lambda g: (start // batch + g, 0, 0)
    plain = lambda g: (g, 0, 0)
    smem = pl.BlockSpec(memory_space=pltpu.SMEM)
    parts, arrays = [], []
    for held, n, lead in pieces:
        parts.append((runs_of(held, n, len(arrays)), lead))
        arrays.extend(held)
    keys = 128 * sum(a.shape[0] for a in arrays)
    begin = state is None
    given, given_specs = [], []
    if not begin:
        given = list(state[:2])
        given_specs = [pl.BlockSpec((batch, tok, width), here), pl.BlockSpec((batch, tok, 256), here)]
    if finish:
        outs = jax.ShapeDtypeStruct((size, tok, width + 128), BF16)
        out_specs = pl.BlockSpec((batch, tok, width + 128), plain)
        scratch = [pltpu.VMEM((batch, tok, width), F32), pltpu.VMEM((batch, tok, 256), F32)]
    else:
        outs = [
            jax.ShapeDtypeStruct((size, tok, width), F32),
            jax.ShapeDtypeStruct((size, tok, 256), F32),
            jax.ShapeDtypeStruct((size,), jnp.int32),
        ]
        out_specs = [pl.BlockSpec((batch, tok, width), plain), pl.BlockSpec((batch, tok, 256), plain), smem]
        scratch = []
    return pl.pallas_call(
        functools.partial(attend_kernel, parts, start, begin, finish, scale),
        grid=(size // batch,),
        in_specs=[smem]
        + ([] if begin else [smem])
        + [pl.BlockSpec((batch, tok, width), here)]
        + given_specs
        + [whole(a.shape) for a in arrays],
        out_specs=out_specs,
        out_shape=outs,
        scratch_shapes=scratch + [pltpu.VMEM((tok, 256), BF16)],
        compiler_params=pltpu.CompilerParams(vmem_limit_bytes=VMEM),
        cost_estimate=pl.CostEstimate(
            flops=4 * size * tok * width * keys,
            bytes_accessed=size * tok * width * 12,
            transcendentals=size * tok * (width // 128) * keys,
        ),
    )(mask, *([] if begin else [state[2]]), queries, *given, *arrays)


def merge(parts, gate):
    tok, width = parts[0].shape[1], gate.shape[1]
    return pl.pallas_call(
        functools.partial(merge_kernel, len(parts)),
        out_shape=jax.ShapeDtypeStruct((1, tok, width), BF16),
        compiler_params=pltpu.CompilerParams(vmem_limit_bytes=VMEM),
    )(*parts, gate)


def swap(value, axis, flip):
    return lax.ppermute(value, axis, [(i, i ^ flip) for i in range(lax.axis_size(axis))])


def partner(value, axes):
    sizes = [lax.axis_size(axis) for axis in axes]
    pairs = []
    for place in itertools.product(*[range(size) for size in sizes]):
        to = [at ^ 1 for at in place]
        pairs.append(tuple(functools.reduce(lambda i, part: i * part[1] + part[0], zip(p, sizes), 0) for p in (place, to)))
    return lax.ppermute(value, axes, pairs)


def mirror(value, axis):
    size = lax.axis_size(axis)
    return lax.ppermute(value, axis, [(i, size - 1 - i) for i in range(size)])


def shards(query, key, value, noise_step, span_mask, gate_weight):
    tie = lax.optimization_barrier
    own = jnp.concatenate([key, value], axis=2)
    own, query = tie((own, query))
    others = [swap(own, "span", by) for by in (1, 2, 3)]
    beside = partner(query, ("x",))
    across = mirror(own, "x")
    along = partner(query, ("zl",))
    others, beside, across, query = tie((others, beside, across, query))
    slots = jnp.concatenate(others, axis=0)
    n = slots.shape[0]
    both = jnp.concatenate([own, across], axis=0)
    c1, c2 = swap(both, "y", 1), mirror(both, "y")
    a0 = jnp.concatenate([slots, mirror(slots, "x")], axis=0)
    queries = jnp.concatenate([partner(query, ("x", "zl")), along, beside, query], axis=0)
    a0, c1, c2, queries = tie((a0, c1, c2, queries))
    early = jnp.concatenate([own, c1[:1], c2[:1], a0[:n], across, c1[1:], c2[1:], a0[n:]], axis=0)
    a1, a2 = swap(a0, "y", 1), mirror(a0, "y")
    b0 = swap(early, "core", 1)
    state = attend(span_mask, queries, 0, 4, [([early, b0], n + 3, 3)], None, False, 4)
    a1, a2, state = tie((a1, a2, state))
    a3 = [
        mirror(jnp.concatenate([c1[:1], a1[:n]], axis=0), "y"),
        swap(jnp.concatenate([c2[1:], a2[n:]], axis=0), "y", 1),
    ]
    b1, b2 = swap(a1, "core", 1), swap(a2, "core", 1)
    middle = ([a1, a2, b1, b2], n, 0)
    rest = attend(span_mask, queries, 0, 3, [middle], state, False, 3)
    a3, rest, noise_step = tie((a3, rest, noise_step))
    a3 = jnp.concatenate(a3, axis=0)
    b3 = swap(a3, "core", 1)
    gate = noise_gate(noise_step, gate_weight, gate_weight.shape[0])
    late = ([a3, b3], n + 1, 1)
    rest = attend(span_mask, queries, 0, 3, [late], rest, True, 3)
    state, rest, gate = tie((state, rest, gate))
    opposite = partner(rest[0:1], ("x", "zl"))
    sides = [partner(rest[1:2], ("zl",)), partner(rest[2:3], ("x",))]
    near = attend(span_mask, queries, 3, 1, [middle, late], state, True)
    opposite, sides, near = tie((opposite, sides, near))
    return merge([near, opposite, *sides], gate)


def solution(mesh):
    fine = Mesh(mesh.devices.reshape(4, 4, 4, 2, 2), ("span", "x", "y", "zl", "core"))
    rows = P("span", ("x", "y", "zl", "core"), None)
    return jax.shard_map(
        shards,
        mesh=fine,
        in_specs=(rows, rows, rows, P(), P(), P()),
        out_specs=rows,
        check_vma=False,
    )
```

```python
import functools
import itertools
import math

import jax
import jax.numpy as jnp
from jax import lax
from jax.experimental import pallas as pl
from jax.experimental.pallas import tpu as pltpu
from jax.sharding import Mesh, PartitionSpec as P

STEPS = 64
NT = (((1,), (1,)), ((), ()))
F32 = jnp.float32
BF16 = jnp.bfloat16
SUM_LOW = 2.0**-80
SUM_HIGH = 2.0**100
VMEM = 24 << 20


def noise_gate(step_now, gate_weight, embed_width):
    half = embed_width // 2
    freqs = jnp.exp(-math.log(10000.0) * jnp.arange(half, dtype=F32) / half)
    angles = step_now.astype(F32)[:, None] * (1000.0 / STEPS) * freqs[None, :]
    embed = jnp.concatenate([jnp.cos(angles), jnp.sin(angles)], axis=1)
    return jax.nn.sigmoid(jnp.dot(embed, gate_weight, precision=lax.Precision.HIGHEST))


def lane_of(rows):
    return lax.broadcasted_iota(jnp.int32, (rows, 128), 1)


def allowed_spans(mask_ref):
    here = lax.axis_index("span")
    may = [jnp.where(mask_ref[here, here ^ by] > 0, 1, 0) for by in (1, 2, 3)]

    def place(j):
        first = jnp.where(may[0] > 0, 0, jnp.where(may[1] > 0, 1, 2))
        second = jnp.where(may[0] * may[1] > 0, 1, 2)
        return jnp.where(j == 0, first, jnp.where(j == 1, second, 2))

    return may[0] + may[1] + may[2], place


def add_blocks(count, pick, start, q_ref, blocks, acc_ref, stat_ref, scale):
    tok = q_ref.shape[1]
    heads = q_ref.shape[2] // 128
    pair = 2 if heads % 2 == 0 else 1
    groups = [blocks[i : i + 8] for i in range(0, len(blocks), 8)]
    steps = [(g, h, i) for g in range(acc_ref.shape[0]) for h in range(heads // pair) for i in range(len(groups))]
    lane = lane_of(tok)

    def rows(g, h):
        parts = [q_ref[start + g, :, (h * pair + j) * 128 : (h * pair + j + 1) * 128] for j in range(pair)]
        return jnp.concatenate(parts, axis=0)

    def slot(s, carry):
        s = pick(s)

        def part(i, low):
            return jnp.concatenate([ref[first + s, :, low : low + 128] for ref, first in groups[i]], axis=0)

        def score(step):
            g, h, i = step
            return lax.dot_general(rows(g, h), part(i, 0), NT, preferred_element_type=F32)

        now = score(steps[0])
        total = None
        for at, (g, h, i) in enumerate(steps):
            later = score(steps[at + 1]) if at + 1 < len(steps) else None
            probs = jnp.exp2(now * scale).astype(BF16)
            values = part(i, 128)
            both = jnp.concatenate([values, jnp.ones_like(values)], axis=1)
            update = jnp.dot(probs, both, preferred_element_type=F32)
            total = update if i == 0 else total + update
            if i == len(groups) - 1:
                for j in range(pair):
                    head = h * pair + j
                    mine = total[j * tok : (j + 1) * tok]
                    acc_ref[g, :, head * 128 : (head + 1) * 128] += mine[:, :128]
                    stat_ref[g, :, :128] = jnp.where(lane == head, stat_ref[g, :, :128] + mine[:, 128:], stat_ref[g, :, :128])
            now = later
        return carry

    lax.fori_loop(0, count, slot, 0)


def add_blocks_slow(count, pick, start, q_ref, blocks, acc_ref, stat_ref, block_ref, scale, g):
    tok = q_ref.shape[1]
    heads = q_ref.shape[2] // 128
    lane = lane_of(tok)

    def head(h, carry):
        cols = pl.ds(pl.multiple_of(h * 128, 128), 128)
        scores = lax.dot_general(q_ref[start + g, :, cols], block_ref[:, :128], NT, preferred_element_type=F32) * scale
        sums = stat_ref[g, :, :128]
        tops = stat_ref[g, :, 128:]
        old = jnp.max(jnp.where(lane == h, tops, -jnp.inf), axis=1, keepdims=True)
        new = jnp.maximum(old, jnp.max(scores, axis=1, keepdims=True))
        back = jnp.exp2(old - new)
        probs = jnp.exp2(scores - new)
        update = jnp.dot(probs.astype(BF16), block_ref[:, 128:], preferred_element_type=F32)
        acc_ref[g, :, cols] = acc_ref[g, :, cols] * back + update
        total = sums * back + jnp.sum(probs, axis=1, keepdims=True)
        stat_ref[g, :, :128] = jnp.where(lane == h, total, sums)
        stat_ref[g, :, 128:] = jnp.where(lane == h, new, tops)
        return carry

    def one(b, carry):
        for i, (ref, first) in enumerate(blocks):

            @pl.when(lax.rem(b, len(blocks)) == i)
            def _(ref=ref, first=first):
                block_ref[...] = ref[first + pick(lax.div(b, len(blocks)))]

        lax.fori_loop(0, heads, head, 0)
        return carry

    lax.fori_loop(0, count * len(blocks), one, 0)


def attend_kernel(parts, start, begin, finish, scale, mask_ref, *refs):
    refs = list(refs)
    block_ref = refs.pop()
    flag_in = None if begin else refs.pop(0)
    q_ref = refs.pop(0)
    acc_in, stat_in = (None, None) if begin else (refs.pop(0), refs.pop(0))
    out_ref = None
    if finish:
        out_ref, acc_ref, stat_ref = refs[-3:]
    else:
        acc_ref, stat_ref, flag_out = refs[-3:]
    others, place = allowed_spans(mask_ref)
    todo = []
    for runs, lead in parts:
        pick = lambda s, lead=lead: jnp.where(s < lead, s, lead + place(s - lead))
        todo.append(([(refs[i], first) for i, first in runs], lead + others, pick))
    size, tok = acc_ref.shape[:2]
    heads = q_ref.shape[2] // 128
    lane = lane_of(tok)
    if begin:
        acc_ref[...] = jnp.zeros_like(acc_ref)
        stat_ref[...] = jnp.zeros_like(stat_ref)
    else:
        acc_ref[...] = acc_in[start : start + size]
        stat_ref[...] = stat_in[start : start + size]
    for blocks, count, pick in todo:
        add_blocks(count, pick, start, q_ref, blocks, acc_ref, stat_ref, scale)
    sums = [stat_ref[g, :, :128] for g in range(size)]
    low = functools.reduce(jnp.minimum, sums)
    high = functools.reduce(jnp.maximum, sums)
    good = (low > SUM_LOW) & (high < SUM_HIGH)
    slow = jnp.max(jnp.where((lane < heads) & jnp.logical_not(good), 1.0, 0.0)) > 0.0
    if not begin:
        for g in range(size):
            slow = slow | (flag_in[start + g] > 0)

    @pl.when(slow)
    def _():
        def group(g, carry):
            if begin:
                acc_ref[g] = jnp.zeros(acc_ref.shape[1:], F32)
                stat_ref[g, :, :128] = jnp.zeros((tok, 128), F32)
                stat_ref[g, :, 128:] = jnp.full((tok, 128), -1e30, F32)
            else:
                acc_ref[g] = acc_in[start + g]
                stat_ref[g] = stat_in[start + g]
            for blocks, count, pick in todo:
                add_blocks_slow(count, pick, start, q_ref, blocks, acc_ref, stat_ref, block_ref, scale, g)
            return carry

        lax.fori_loop(0, size, group, 0)

    if not finish:
        for g in range(size):
            flag_out[g] = jnp.where(slow, 1, 0)
        return
    for g in range(size):
        pack(acc_ref, stat_ref, out_ref, g)


def pack(acc_ref, stat_ref, out_ref, g):
    tok = out_ref.shape[1]
    heads = out_ref.shape[2] // 128 - 1
    lane = lane_of(tok)
    sums = jnp.where(lane < heads, stat_ref[g, :, :128], 1.0)
    weight = jnp.log(sums) * (1.0 / math.log(2.0)) + stat_ref[g, :, 128:]
    inverse = 1.0 / sums
    for h in range(heads):
        cols = slice(h * 128, (h + 1) * 128)
        out_ref[g, :, cols] = (acc_ref[g, :, cols] * inverse[:, h : h + 1]).astype(BF16)
    first = weight.astype(BF16).astype(F32)
    second = (weight - first).astype(BF16).astype(F32)
    third = weight - first - second
    packed = jnp.where(lane < 8, first, 0.0)
    packed = packed + pltpu.roll(jnp.where(lane < 8, second, 0.0), 8, 1)
    packed = packed + pltpu.roll(jnp.where(lane < 8, third, 0.0), 16, 1)
    out_ref[g, :, heads * 128 :] = packed.astype(BF16)


def merge_kernel(n, *refs):
    parts, gate_ref, out_ref = refs[:n], refs[n], refs[n + 1]
    tok = out_ref.shape[1]
    heads = out_ref.shape[2] // 128
    rows = lax.broadcasted_iota(jnp.int32, gate_ref.shape, 0)
    mine = jnp.where(rows == lax.axis_index("span"), gate_ref[...], 0.0)
    gate = jnp.sum(mine, axis=0, keepdims=True)
    weights = []
    for ref in parts:
        packed = ref[0, :, heads * 128 :].astype(F32)
        weights.append(packed + pltpu.roll(packed, 120, 1) + pltpu.roll(packed, 112, 1))
    top = functools.reduce(jnp.maximum, weights)
    weights = [jnp.exp2(w - top) for w in weights]
    inverse = 1.0 / functools.reduce(jnp.add, weights)
    weights = [w * inverse for w in weights]
    mixed = []
    square = jnp.zeros((tok, 128), F32)
    for h in range(heads):
        cols = slice(h * 128, (h + 1) * 128)
        value = None
        for ref, w in zip(parts, weights):
            term = ref[0, :, cols].astype(F32) * w[:, h : h + 1]
            value = term if value is None else value + term
        mixed.append(value)
        square = square + value * value
    mean = jnp.sum(square, axis=1, keepdims=True) * (1.0 / (heads * 128))
    factor = lax.rsqrt(mean + 1e-06)
    for h in range(heads):
        cols = slice(h * 128, (h + 1) * 128)
        out_ref[0, :, cols] = (gate[:, cols] * (mixed[h] * factor)).astype(BF16)


def runs_of(arrays, n, at):
    return [(at + i, f) for i, a in enumerate(arrays) for f in range(0, a.shape[0], n)]


def attend(mask, queries, start, size, pieces, state, finish, costly=True):
    tok, width = queries.shape[1:]
    scale = 128 ** (-0.5) * math.log2(math.e)
    vmem = pl.BlockSpec(memory_space=pltpu.VMEM)
    smem = pl.BlockSpec(memory_space=pltpu.SMEM)
    parts, arrays = [], []
    for held, n, lead in pieces:
        parts.append((runs_of(held, n, len(arrays)), lead))
        arrays.extend(held)
    keys = 128 * sum(a.shape[0] for a in arrays)
    begin = state is None
    given, given_specs = [], []
    if not begin:
        given = list(state[:2])
        given_specs = [vmem, vmem]
    if finish:
        outs = jax.ShapeDtypeStruct((size, tok, width + 128), BF16)
        out_specs = vmem
        scratch = [pltpu.VMEM((size, tok, width), F32), pltpu.VMEM((size, tok, 256), F32)]
    else:
        outs = [
            jax.ShapeDtypeStruct((size, tok, width), F32),
            jax.ShapeDtypeStruct((size, tok, 256), F32),
            jax.ShapeDtypeStruct((size,), jnp.int32),
        ]
        out_specs = [vmem, vmem, smem]
        scratch = []
    return pl.pallas_call(
        functools.partial(attend_kernel, parts, start, begin, finish, scale),
        in_specs=[smem]
        + ([] if begin else [smem])
        + [vmem]
        + given_specs
        + [vmem] * len(arrays),
        out_specs=out_specs,
        out_shape=outs,
        scratch_shapes=scratch + [pltpu.VMEM((tok, 256), BF16)],
        compiler_params=pltpu.CompilerParams(vmem_limit_bytes=VMEM),
        cost_estimate=pl.CostEstimate(
            flops=4 * size * tok * width * keys if costly else 0,
            bytes_accessed=size * tok * width * 12 if costly else 0,
            transcendentals=size * tok * (width // 128) * keys if costly else 0,
        ),
    )(mask, *([] if begin else [state[2]]), queries, *given, *arrays)


def merge(parts, gate):
    tok, width = parts[0].shape[1], gate.shape[1]
    return pl.pallas_call(
        functools.partial(merge_kernel, len(parts)),
        out_shape=jax.ShapeDtypeStruct((1, tok, width), BF16),
        compiler_params=pltpu.CompilerParams(vmem_limit_bytes=VMEM),
    )(*parts, gate)


def swap(value, axis, flip):
    return lax.ppermute(value, axis, [(i, i ^ flip) for i in range(lax.axis_size(axis))])


def partner(value, axes):
    sizes = [lax.axis_size(axis) for axis in axes]
    pairs = []
    for place in itertools.product(*[range(size) for size in sizes]):
        to = [at ^ 1 for at in place]
        pairs.append(tuple(functools.reduce(lambda i, part: i * part[1] + part[0], zip(p, sizes), 0) for p in (place, to)))
    return lax.ppermute(value, axes, pairs)


def mirror(value, axis):
    size = lax.axis_size(axis)
    return lax.ppermute(value, axis, [(i, size - 1 - i) for i in range(size)])


def shards(query, key, value, noise_step, span_mask, gate_weight):
    tie = lax.optimization_barrier
    own = jnp.concatenate([key, value], axis=2)
    own, query = tie((own, query))
    others = [swap(own, "span", by) for by in (1, 2, 3)]
    beside = partner(query, ("x",))
    across = mirror(own, "x")
    both = jnp.concatenate([own, across], axis=0)
    c1, c2 = swap(both, "y", 1), mirror(both, "y")
    along = partner(query, ("zl",))
    others, beside, query = tie((others, beside, query))
    slots = jnp.concatenate(others, axis=0)
    n = slots.shape[0]
    a0 = jnp.concatenate([slots, mirror(slots, "x")], axis=0)
    queries = jnp.concatenate([partner(query, ("x", "zl")), along, beside, query], axis=0)
    a0, c1, c2, queries = tie((a0, c1, c2, queries))
    early = jnp.concatenate([own, c1[:1], c2[:1], a0[:n], across, c1[1:], c2[1:], a0[n:]], axis=0)
    a1, a2 = swap(a0, "y", 1), mirror(a0, "y")
    b0 = swap(early, "core", 1)
    state = attend(span_mask, queries, 0, 4, [([early, b0], n + 3, 3)], None, False)
    a1, a2, state = tie((a1, a2, state))
    a3 = [
        mirror(jnp.concatenate([c1[:1], a1[:n]], axis=0), "y"),
        swap(jnp.concatenate([c2[1:], a2[n:]], axis=0), "y", 1),
    ]
    b1, b2 = swap(a1, "core", 1), swap(a2, "core", 1)
    middle = ([a1, a2, b1, b2], n, 0)
    rest = attend(span_mask, queries, 0, 3, [middle], state, False)
    a3, rest, noise_step = tie((a3, rest, noise_step))
    a3 = jnp.concatenate(a3, axis=0)
    b3 = swap(a3, "core", 1)
    gate = noise_gate(noise_step, gate_weight, gate_weight.shape[0])
    late = ([a3, b3], n + 1, 1)
    opposite = attend(span_mask, queries, 0, 1, [late], rest, True)
    opposite, rest, gate = tie((opposite, rest, gate))
    opposite = partner(opposite, ("x", "zl"))
    sides = attend(span_mask, queries, 1, 2, [late], rest, True, False)
    state, sides = tie((state, sides))
    sides = [partner(sides[0:1], ("zl",)), partner(sides[1:2], ("x",))]
    near = attend(span_mask, queries, 3, 1, [middle, late], state, True, False)
    opposite, sides, near = tie((opposite, sides, near))
    return merge([near, opposite, *sides], gate)


def solution(mesh):
    fine = Mesh(mesh.devices.reshape(4, 4, 4, 2, 2), ("span", "x", "y", "zl", "core"))
    rows = P("span", ("x", "y", "zl", "core"), None)
    return jax.shard_map(
        shards,
        mesh=fine,
        in_specs=(rows, rows, rows, P(), P(), P()),
        out_specs=rows,
        check_vma=False,
    )
```

```python
import functools
import itertools
import math

import jax
import jax.numpy as jnp
from jax import lax
from jax.experimental import pallas as pl
from jax.experimental.pallas import tpu as pltpu
from jax.sharding import Mesh, PartitionSpec as P

STEPS = 64
NT = (((1,), (1,)), ((), ()))
F32 = jnp.float32
BF16 = jnp.bfloat16
SUM_LOW = 2.0**-80
SUM_HIGH = 2.0**100
VMEM = 24 << 20


def noise_gate(step_now, gate_weight, embed_width):
    half = embed_width // 2
    freqs = jnp.exp(-math.log(10000.0) * jnp.arange(half, dtype=F32) / half)
    angles = step_now.astype(F32)[:, None] * (1000.0 / STEPS) * freqs[None, :]
    embed = jnp.concatenate([jnp.cos(angles), jnp.sin(angles)], axis=1)
    return jax.nn.sigmoid(jnp.dot(embed, gate_weight, precision=lax.Precision.HIGHEST))


def lane_of(rows):
    return lax.broadcasted_iota(jnp.int32, (rows, 128), 1)


def allowed_spans(mask_ref):
    here = lax.axis_index("span")
    may = [jnp.where(mask_ref[here, here ^ by] > 0, 1, 0) for by in (1, 2, 3)]

    def place(j):
        first = jnp.where(may[0] > 0, 0, jnp.where(may[1] > 0, 1, 2))
        second = jnp.where(may[0] * may[1] > 0, 1, 2)
        return jnp.where(j == 0, first, jnp.where(j == 1, second, 2))

    return may[0] + may[1] + may[2], place


def add_blocks(count, pick, start, q_ref, blocks, acc_ref, stat_ref, scale):
    tok = q_ref.shape[1]
    heads = q_ref.shape[2] // 128
    pair = 2 if heads % 2 == 0 else 1
    groups = [blocks[i : i + 8] for i in range(0, len(blocks), 8)]
    steps = [(g, h, i) for g in range(acc_ref.shape[0]) for h in range(heads // pair) for i in range(len(groups))]
    lane = lane_of(tok)

    def rows(g, h):
        parts = [q_ref[start + g, :, (h * pair + j) * 128 : (h * pair + j + 1) * 128] for j in range(pair)]
        return jnp.concatenate(parts, axis=0)

    def slot(s, carry):
        s = pick(s)

        def part(i, low):
            return jnp.concatenate([ref[first + s, :, low : low + 128] for ref, first in groups[i]], axis=0)

        def score(step):
            g, h, i = step
            return lax.dot_general(rows(g, h), part(i, 0), NT, preferred_element_type=F32)

        now = score(steps[0])
        total = None
        for at, (g, h, i) in enumerate(steps):
            later = score(steps[at + 1]) if at + 1 < len(steps) else None
            probs = jnp.exp2(now * scale).astype(BF16)
            values = part(i, 128)
            both = jnp.concatenate([values, jnp.ones_like(values)], axis=1)
            update = jnp.dot(probs, both, preferred_element_type=F32)
            total = update if i == 0 else total + update
            if i == len(groups) - 1:
                for j in range(pair):
                    head = h * pair + j
                    mine = total[j * tok : (j + 1) * tok]
                    acc_ref[g, :, head * 128 : (head + 1) * 128] += mine[:, :128]
                    stat_ref[g, :, :128] = jnp.where(lane == head, stat_ref[g, :, :128] + mine[:, 128:], stat_ref[g, :, :128])
            now = later
        return carry

    lax.fori_loop(0, count, slot, 0)


def add_blocks_slow(count, pick, start, q_ref, blocks, acc_ref, stat_ref, block_ref, scale, g):
    tok = q_ref.shape[1]
    heads = q_ref.shape[2] // 128
    lane = lane_of(tok)

    def head(h, carry):
        cols = pl.ds(pl.multiple_of(h * 128, 128), 128)
        scores = lax.dot_general(q_ref[start + g, :, cols], block_ref[:, :128], NT, preferred_element_type=F32) * scale
        sums = stat_ref[g, :, :128]
        tops = stat_ref[g, :, 128:]
        old = jnp.max(jnp.where(lane == h, tops, -jnp.inf), axis=1, keepdims=True)
        new = jnp.maximum(old, jnp.max(scores, axis=1, keepdims=True))
        back = jnp.exp2(old - new)
        probs = jnp.exp2(scores - new)
        update = jnp.dot(probs.astype(BF16), block_ref[:, 128:], preferred_element_type=F32)
        acc_ref[g, :, cols] = acc_ref[g, :, cols] * back + update
        total = sums * back + jnp.sum(probs, axis=1, keepdims=True)
        stat_ref[g, :, :128] = jnp.where(lane == h, total, sums)
        stat_ref[g, :, 128:] = jnp.where(lane == h, new, tops)
        return carry

    def one(b, carry):
        for i, (ref, first) in enumerate(blocks):

            @pl.when(lax.rem(b, len(blocks)) == i)
            def _(ref=ref, first=first):
                block_ref[...] = ref[first + pick(lax.div(b, len(blocks)))]

        lax.fori_loop(0, heads, head, 0)
        return carry

    lax.fori_loop(0, count * len(blocks), one, 0)


def attend_kernel(parts, start, begin, finish, scale, mask_ref, *refs):
    refs = list(refs)
    block_ref = refs.pop()
    flag_in = None if begin else refs.pop(0)
    q_ref = refs.pop(0)
    acc_in, stat_in = (None, None) if begin else (refs.pop(0), refs.pop(0))
    out_ref = None
    if finish:
        out_ref, acc_ref, stat_ref = refs[-3:]
    else:
        acc_ref, stat_ref, flag_out = refs[-3:]
    others, place = allowed_spans(mask_ref)
    todo = []
    for runs, lead in parts:
        pick = lambda s, lead=lead: jnp.where(s < lead, s, lead + place(s - lead))
        todo.append(([(refs[i], first) for i, first in runs], lead + others, pick))
    size, tok = acc_ref.shape[:2]
    heads = q_ref.shape[2] // 128
    lane = lane_of(tok)
    if begin:
        acc_ref[...] = jnp.zeros_like(acc_ref)
        stat_ref[...] = jnp.zeros_like(stat_ref)
    else:
        acc_ref[...] = acc_in[start : start + size]
        stat_ref[...] = stat_in[start : start + size]
    for blocks, count, pick in todo:
        add_blocks(count, pick, start, q_ref, blocks, acc_ref, stat_ref, scale)
    sums = [stat_ref[g, :, :128] for g in range(size)]
    low = functools.reduce(jnp.minimum, sums)
    high = functools.reduce(jnp.maximum, sums)
    good = (low > SUM_LOW) & (high < SUM_HIGH)
    slow = jnp.max(jnp.where((lane < heads) & jnp.logical_not(good), 1.0, 0.0)) > 0.0
    if not begin:
        for g in range(size):
            slow = slow | (flag_in[start + g] > 0)

    @pl.when(slow)
    def _():
        def group(g, carry):
            if begin:
                acc_ref[g] = jnp.zeros(acc_ref.shape[1:], F32)
                stat_ref[g, :, :128] = jnp.zeros((tok, 128), F32)
                stat_ref[g, :, 128:] = jnp.full((tok, 128), -1e30, F32)
            else:
                acc_ref[g] = acc_in[start + g]
                stat_ref[g] = stat_in[start + g]
            for blocks, count, pick in todo:
                add_blocks_slow(count, pick, start, q_ref, blocks, acc_ref, stat_ref, block_ref, scale, g)
            return carry

        lax.fori_loop(0, size, group, 0)

    if not finish:
        for g in range(size):
            flag_out[g] = jnp.where(slow, 1, 0)
        return
    for g in range(size):
        pack(acc_ref, stat_ref, out_ref, g)


def pack(acc_ref, stat_ref, out_ref, g):
    tok = out_ref.shape[1]
    heads = out_ref.shape[2] // 128 - 1
    lane = lane_of(tok)
    sums = jnp.where(lane < heads, stat_ref[g, :, :128], 1.0)
    weight = jnp.log(sums) * (1.0 / math.log(2.0)) + stat_ref[g, :, 128:]
    inverse = 1.0 / sums
    for h in range(heads):
        cols = slice(h * 128, (h + 1) * 128)
        out_ref[g, :, cols] = (acc_ref[g, :, cols] * inverse[:, h : h + 1]).astype(BF16)
    first = weight.astype(BF16).astype(F32)
    second = (weight - first).astype(BF16).astype(F32)
    third = weight - first - second
    packed = jnp.where(lane < 8, first, 0.0)
    packed = packed + pltpu.roll(jnp.where(lane < 8, second, 0.0), 8, 1)
    packed = packed + pltpu.roll(jnp.where(lane < 8, third, 0.0), 16, 1)
    out_ref[g, :, heads * 128 :] = packed.astype(BF16)


def merge_kernel(n, *refs):
    parts, gate_ref, out_ref = refs[:n], refs[n], refs[n + 1]
    tok = out_ref.shape[1]
    heads = out_ref.shape[2] // 128
    rows = lax.broadcasted_iota(jnp.int32, gate_ref.shape, 0)
    mine = jnp.where(rows == lax.axis_index("span"), gate_ref[...], 0.0)
    gate = jnp.sum(mine, axis=0, keepdims=True)
    weights = []
    for ref in parts:
        packed = ref[0, :, heads * 128 :].astype(F32)
        weights.append(packed + pltpu.roll(packed, 120, 1) + pltpu.roll(packed, 112, 1))
    top = functools.reduce(jnp.maximum, weights)
    weights = [jnp.exp2(w - top) for w in weights]
    inverse = 1.0 / functools.reduce(jnp.add, weights)
    weights = [w * inverse for w in weights]
    mixed = []
    square = jnp.zeros((tok, 128), F32)
    for h in range(heads):
        cols = slice(h * 128, (h + 1) * 128)
        value = None
        for ref, w in zip(parts, weights):
            term = ref[0, :, cols].astype(F32) * w[:, h : h + 1]
            value = term if value is None else value + term
        mixed.append(value)
        square = square + value * value
    mean = jnp.sum(square, axis=1, keepdims=True) * (1.0 / (heads * 128))
    factor = lax.rsqrt(mean + 1e-06)
    for h in range(heads):
        cols = slice(h * 128, (h + 1) * 128)
        out_ref[0, :, cols] = (gate[:, cols] * (mixed[h] * factor)).astype(BF16)


def runs_of(arrays, n, at):
    return [(at + i, f) for i, a in enumerate(arrays) for f in range(0, a.shape[0], n)]


def attend(mask, queries, start, size, pieces, state, finish, costly=True):
    tok, width = queries.shape[1:]
    scale = 128 ** (-0.5) * math.log2(math.e)
    vmem = pl.BlockSpec(memory_space=pltpu.VMEM)
    smem = pl.BlockSpec(memory_space=pltpu.SMEM)
    parts, arrays = [], []
    for held, n, lead in pieces:
        parts.append((runs_of(held, n, len(arrays)), lead))
        arrays.extend(held)
    keys = 128 * sum(a.shape[0] for a in arrays)
    begin = state is None
    given, given_specs = [], []
    if not begin:
        given = list(state[:2])
        given_specs = [vmem, vmem]
    if finish:
        outs = jax.ShapeDtypeStruct((size, tok, width + 128), BF16)
        out_specs = vmem
        scratch = [pltpu.VMEM((size, tok, width), F32), pltpu.VMEM((size, tok, 256), F32)]
    else:
        outs = [
            jax.ShapeDtypeStruct((size, tok, width), F32),
            jax.ShapeDtypeStruct((size, tok, 256), F32),
            jax.ShapeDtypeStruct((size,), jnp.int32),
        ]
        out_specs = [vmem, vmem, smem]
        scratch = []
    return pl.pallas_call(
        functools.partial(attend_kernel, parts, start, begin, finish, scale),
        in_specs=[smem]
        + ([] if begin else [smem])
        + [vmem]
        + given_specs
        + [vmem] * len(arrays),
        out_specs=out_specs,
        out_shape=outs,
        scratch_shapes=scratch + [pltpu.VMEM((tok, 256), BF16)],
        compiler_params=pltpu.CompilerParams(vmem_limit_bytes=VMEM),
        cost_estimate=pl.CostEstimate(
            flops=4 * size * tok * width * keys if costly else 0,
            bytes_accessed=size * tok * width * 12 if costly else 0,
            transcendentals=size * tok * (width // 128) * keys if costly else 0,
        ),
    )(mask, *([] if begin else [state[2]]), queries, *given, *arrays)


def merge(parts, gate):
    tok, width = parts[0].shape[1], gate.shape[1]
    return pl.pallas_call(
        functools.partial(merge_kernel, len(parts)),
        out_shape=jax.ShapeDtypeStruct((1, tok, width), BF16),
        compiler_params=pltpu.CompilerParams(vmem_limit_bytes=VMEM),
    )(*parts, gate)


def swap(value, axis, flip):
    return lax.ppermute(value, axis, [(i, i ^ flip) for i in range(lax.axis_size(axis))])


def partner(value, axes):
    sizes = [lax.axis_size(axis) for axis in axes]
    pairs = []
    for place in itertools.product(*[range(size) for size in sizes]):
        to = [at ^ 1 for at in place]
        pairs.append(tuple(functools.reduce(lambda i, part: i * part[1] + part[0], zip(p, sizes), 0) for p in (place, to)))
    return lax.ppermute(value, axes, pairs)


def mirror(value, axis):
    size = lax.axis_size(axis)
    return lax.ppermute(value, axis, [(i, size - 1 - i) for i in range(size)])


def shards(query, key, value, noise_step, span_mask, gate_weight):
    tie = lax.optimization_barrier
    own = jnp.concatenate([key, value], axis=2)
    own, query = tie((own, query))
    others = [swap(own, "span", by) for by in (3, 2, 1)][::-1]
    beside = partner(query, ("x",))
    across = mirror(own, "x")
    both = jnp.concatenate([own, across], axis=0)
    c1, c2 = swap(both, "y", 1), mirror(both, "y")
    along = partner(query, ("zl",))
    others, beside, query = tie((others, beside, query))
    slots = jnp.concatenate(others, axis=0)
    n = slots.shape[0]
    a0 = jnp.concatenate([slots, mirror(slots, "x")], axis=0)
    queries = jnp.concatenate([partner(query, ("x", "zl")), along, beside, query], axis=0)
    a0, c1, c2, queries = tie((a0, c1, c2, queries))
    early = jnp.concatenate([own, c1[:1], c2[:1], a0[:n], across, c1[1:], c2[1:], a0[n:]], axis=0)
    a1, a2 = swap(a0, "y", 1), mirror(a0, "y")
    b0 = swap(early, "core", 1)
    state = attend(span_mask, queries, 0, 4, [([early, b0], n + 3, 3)], None, False)
    a1, a2, state = tie((a1, a2, state))
    a3 = [
        mirror(jnp.concatenate([c1[:1], a1[:n]], axis=0), "y"),
        swap(jnp.concatenate([c2[1:], a2[n:]], axis=0), "y", 1),
    ]
    b1, b2 = swap(a1, "core", 1), swap(a2, "core", 1)
    middle = ([a1, a2, b1, b2], n, 0)
    rest = attend(span_mask, queries, 0, 3, [middle], state, False)
    a3, rest, noise_step = tie((a3, rest, noise_step))
    a3 = jnp.concatenate(a3, axis=0)
    b3 = swap(a3, "core", 1)
    gate = noise_gate(noise_step, gate_weight, gate_weight.shape[0])
    late = ([a3, b3], n + 1, 1)
    opposite = attend(span_mask, queries, 0, 1, [late], rest, True)
    opposite, rest, gate = tie((opposite, rest, gate))
    opposite = partner(opposite, ("x", "zl"))
    sides = attend(span_mask, queries, 1, 2, [late], rest, True, False)
    state, sides = tie((state, sides))
    sides = [partner(sides[0:1], ("zl",)), partner(sides[1:2], ("x",))]
    near = attend(span_mask, queries, 3, 1, [middle, late], state, True, False)
    opposite, sides, near = tie((opposite, sides, near))
    return merge([near, opposite, *sides], gate)


def solution(mesh):
    fine = Mesh(mesh.devices.reshape(4, 4, 4, 2, 2), ("span", "x", "y", "zl", "core"))
    rows = P("span", ("x", "y", "zl", "core"), None)
    return jax.shard_map(
        shards,
        mesh=fine,
        in_specs=(rows, rows, rows, P(), P(), P()),
        out_specs=rows,
        check_vma=False,
    )
```
